512 devices in a mesh: section: 16 (over z), tp: 8 (over x, core), rep: 4 (over y).
Axes of the slice: x: 4, y: 4, z: 16, core: 2. Of those that a mesh axis runs over, the one named last changes fastest.
Arguments:
- pool: bfloat16 [512, 128, 2, 2048], P(('rep', 'section', 'tp')), parts along dimension 0, may hold values from -6 to 6
- queries: bfloat16 [16, 32, 16384], P('section', 'rep', 'tp'), parts along dimension 1, may hold values from -4 to 4
- new_kv: bfloat16 [16, 32, 2, 1024], P('section', 'rep', None, 'tp'), parts along dimension 1, may hold values from -4 to 4
- stream_in: bfloat16 [32, 16384], P('rep', 'tp'), parts along dimension 0, may hold values from -4 to 4
- page_map: int32 [512], P('rep'), parts along dimension 0, may hold values from 0 to 127, each once
- page_counts: int32 [32], P('rep'), parts along dimension 0, may hold values from 1 to 32, 128 in all
- last_fill: int32 [32], P('rep'), parts along dimension 0, may hold values from 1 to 16
Outputs:
- attended: bfloat16 [16, 32, 16384], P('section', 'rep', 'tp'), parts along dimension 1
The draws below stay inside these ranges and needn't reach their ends.
There are 4 independent parts, one for each index of `rep`. The reference program is written for one: setup_inputs(seed, part) draws one part's arguments, and reference() takes and returns one part's arrays. A program takes and returns all parts, laid end to end along the dimension named above; each array names one. Nothing has to cross between parts.
Inputs may be any that keep to these rules, and one draw needn't show every extreme that they name: Request r owns the pool pages page_map[o_r], ..., page_map[o_r + page_counts[r] - 1], o_r being the sum of page_counts over earlier requests; every pool page belongs to exactly one request. `page_counts`: the counts sum to 128.
All inputs are finite; a program needn't handle non-finite values.
Results may differ from the reference program's by a relative error of at most 0.019.
Values may be sent and summed in bfloat16 or wider, within the bound.
A program may use at most 64 MiB of HBM per device.

```python
import math
import jax
import jax.numpy as jnp
import numpy as np
from jax import lax

HD = 128
GROUP = 16
PAGE = 16
MAXP = 32
LAYERS = 16
KVH = 8
HEADS = 128
SLOTS = 128
ROWS = 8
PAGES = 128
N_SECTION = 16
N_TP = 8


def draw_pool(key, part):
    key = jax.random.fold_in(key, 11)
    shape = (PAGES, SLOTS, 2, PAGE * HD)
    sample = jnp.clip(jax.random.normal(key, shape, jnp.float32), -6.0, 6.0)
    return sample.astype(jnp.bfloat16)


def draw_queries(key, part):
    key = jax.random.fold_in(key, 23)
    shape = (LAYERS, ROWS, HEADS * HD)
    sample = jnp.clip(jax.random.normal(key, shape, jnp.float32), -4.0, 4.0)
    return sample.astype(jnp.bfloat16)


def set_ends(result, stream_key, smallest, high):
    place = [jax.random.randint(jax.random.fold_in(stream_key, axis), (), 0, length) for axis, length in enumerate(result.shape)]
    main_axis = result.shape.index(max(result.shape))
    beside = place[:main_axis] + [(place[main_axis] + 1) % result.shape[main_axis]] + place[main_axis + 1:]
    return result.at[tuple(place)].set(smallest).at[tuple(beside)].set(high)


def level_of(rng, dims, pieces, least, high):
    def one(axis_at, blocks):
        heights = jax.random.uniform(jax.random.fold_in(jax.random.fold_in(rng, 6), axis_at), (blocks,), jnp.float32, least / len(pieces), high / len(pieces))
        return jnp.repeat(jnp.exp(heights), dims[axis_at] // blocks).reshape((-1,) + (1,) * (len(dims) - axis_at - 1))

    loudness = one(*pieces[0])
    for cut in pieces[1:]:
        loudness = loudness * one(*cut)
    return loudness


def length_profile(amount, total, bound, slope):
    weights = [(1 << 20) // math.isqrt(grade ** slope) + 1 for grade in range(2, amount + 1)]
    spare, given = total - bound - (amount - 1), [1] * (amount - 1)
    while spare > 0:
        movable = [i for i in range(amount - 1) if given[i] < bound]
        mass, left = sum([weights[i] for i in movable]), spare
        for i in movable:
            addition = min(bound - given[i], max(1, left * weights[i] // mass), spare)
            given[i] = given[i] + addition
            spare = spare - addition
    return np.array([bound] + given)


def uneven(stream_key, amount, total, bound, slope):
    if amount == 2:
        one = jax.random.randint(stream_key, (), max(1, total - bound), min(bound, total - 1) + 1)
        return jnp.stack([one, total - one])
    sizes = jnp.asarray(length_profile(amount, total, bound, slope), jnp.int32)
    couples = (amount - 1) // 2
    source_of, sink = sizes[1:1 + 2 * couples:2], sizes[2:2 + 2 * couples:2]
    margin = jnp.minimum(source_of - 1, bound - sink)
    shifted = jax.random.randint(jax.random.fold_in(stream_key, 1), (couples,), 0, 1 << 20) % (margin + 1)
    sizes = sizes.at[1:1 + 2 * couples:2].set(source_of - shifted).at[2:2 + 2 * couples:2].set(sink + shifted)
    return sizes[jax.random.permutation(jax.random.fold_in(stream_key, 2), amount)]


def gaussian(stream_key, dims, scale, limit, split=(), held_as=jnp.bfloat16):
    entries = jax.random.normal(stream_key, dims, jnp.float32) * scale
    if len(split) > 0:
        entries = level_of(stream_key, dims, split, -0.22, 0.18) * entries
    return jnp.clip(entries, min=-limit, max=limit).astype(held_as)


def setup_inputs(seed: int = 0, part: int = 0) -> dict:
    seeds = jax.random.split(jax.random.key(seed), 8)
    part_splits = jax.random.split(jax.random.fold_in(seeds[7], part), 8)
    pool = draw_pool(jax.random.fold_in(jax.random.fold_in(seeds[7], part), 71), part)
    queries = draw_queries(jax.random.fold_in(jax.random.fold_in(seeds[7], part), 71), part)
    new_kv = gaussian(part_splits[2], (LAYERS, ROWS, 2, KVH * HD), 1.0, 4.0, ((0, 16), (3, 8)))
    stream_in = gaussian(part_splits[3], (ROWS, HEADS * HD), 1.0, 4.0, ((1, 8),))
    page_map = jax.random.permutation(part_splits[4], PAGES).astype(jnp.int32)
    page_counts = uneven(part_splits[5], ROWS, PAGES, MAXP, 2).astype(jnp.int32)
    last_fill = set_ends(jax.random.randint(part_splits[6], (ROWS,), 1, PAGE + 1), jax.random.fold_in(part_splits[6], 1), 1, PAGE).astype(jnp.int32)
    return dict(pool=pool, queries=queries, new_kv=new_kv, stream_in=stream_in, page_map=page_map, page_counts=page_counts, last_fill=last_fill)


epsilon = 1e-05

def build_tables(page_map, page_counts, last_fill):
    counts = page_counts.astype(jnp.int32)
    offsets = (jnp.cumsum(counts) - counts).astype(jnp.int32)
    column = jnp.arange(MAXP, dtype=jnp.int32)
    position = (offsets[:, None] + jnp.minimum(column[None, :], counts[:, None] - 1)).astype(jnp.int32)
    page_ids = page_map[position]
    length = (counts - 1) * PAGE + last_fill.astype(jnp.int32)
    token_pos = jnp.arange(MAXP * PAGE, dtype=jnp.int32)
    return (page_ids, token_pos[None, :] < length[:, None])

def normed(stream, head_dim):
    values = stream.astype(jnp.float32)
    shaped = values.reshape(values.shape[0], -1, head_dim)
    scaled = shaped * lax.rsqrt(lax.optimization_barrier(jnp.mean(shaped * shaped, axis=-1, keepdims=True)) + epsilon)
    return scaled.reshape(values.shape)

def reference(pool, queries, new_kv, stream_in, page_map, page_counts, last_fill):
    page_ids, live = build_tables(page_map, page_counts, last_fill)
    scale = 1.0 / math.sqrt(HD)
    stream = stream_in
    outputs = []
    live_mask = live[:, None, None, :]
    for layer_idx in range(N_SECTION):
        layer_pages = pool[:, layer_idx * N_TP:(layer_idx + 1) * N_TP]
        gathered = layer_pages[page_ids]
        shaped = gathered.reshape(ROWS, MAXP, N_TP, 2, PAGE, HD).transpose(0, 2, 3, 1, 4, 5)
        shaped = shaped.reshape(ROWS, N_TP, 2, MAXP * PAGE, HD)
        key_rows = shaped[:, :, 0].astype(jnp.float32)
        value_rows = shaped[:, :, 1].astype(jnp.float32)
        query_rows = (queries[layer_idx].astype(jnp.float32) + normed(stream, HD)).astype(jnp.bfloat16)
        query_rows = query_rows.reshape(ROWS, N_TP, GROUP, HD).astype(jnp.float32)
        new_entry = new_kv[layer_idx].reshape(ROWS, 2, N_TP, HD).astype(jnp.float32)
        scores = jnp.einsum('rkgd,rktd->rkgt', query_rows, key_rows) * scale
        own_score = jnp.einsum('rkgd,rkd->rkg', query_rows, new_entry[:, 0]) * scale
        highest = jnp.maximum(lax.optimization_barrier(jnp.max(jnp.where(live_mask, scores, -1e+30), axis=-1)), own_score)
        weights = jnp.where(live_mask, jnp.exp(scores - highest[..., None]), 0.0)
        own_weight = jnp.exp(own_score - highest)
        denominator = lax.optimization_barrier(jnp.sum(weights, axis=-1)) + own_weight
        weights = (weights / denominator[..., None]).astype(jnp.bfloat16)
        own_weight = (own_weight / denominator).astype(jnp.bfloat16)
        mixture = jnp.einsum('rkgt,rktd->rkgd', weights.astype(jnp.float32), value_rows)
        mixture = mixture + own_weight.astype(jnp.float32)[..., None] * new_entry[:, 1][:, :, None, :]
        attended = mixture.astype(jnp.bfloat16).reshape(ROWS, -1)
        outputs.append(attended)
        stream = (stream.astype(jnp.float32) + attended.astype(jnp.float32)).astype(jnp.bfloat16)
    return jnp.stack(outputs)
```

```python
import math

import jax
import jax.numpy as jnp
from jax import lax
from jax.experimental import pallas as pl
from jax.experimental.pallas import tpu as pltpu
from jax.sharding import PartitionSpec as P

HD = 128
PAGE = 16
GROUP = 16
ROWS = 8
EPS = 1e-05
HIDDEN = -1e30
MESH = pl.DeviceIdType.MESH
EXP2_SCALE = math.log2(math.e) / math.sqrt(HD)


def contract_last(a, b):
    return lax.dot_general(a, b, (((1,), (1,)), ((), ())), preferred_element_type=jnp.float32)


def by_group(block):
    wide = block.astype(jnp.float32)
    return jnp.concatenate([wide[:, g * HD : (g + 1) * HD] for g in range(GROUP)], axis=0)


def build_bias(page_map_ref, counts_ref, fill_ref, bias_ref, pages):
    place = lax.broadcasted_iota(jnp.int32, (16, pages), 1)
    row = lax.broadcasted_iota(jnp.int32, (16, pages), 0)
    limit = jnp.zeros((16, pages), jnp.int32)
    first = jnp.int32(0)
    for r in range(ROWS):
        last = first + counts_ref[r] - 1
        here = jnp.where(place < last, PAGE, jnp.where(place == last, fill_ref[r], 0))
        here = jnp.where(place >= first, here, 0)
        limit = jnp.where(row == r, here, limit)
        first = last + 1
    owner = page_map_ref[...] == lax.broadcasted_iota(jnp.int32, (pages, pages), 0)
    limit = contract_last(
        limit.astype(jnp.float32).astype(jnp.bfloat16),
        jnp.where(owner, 1.0, 0.0).astype(jnp.bfloat16),
    ).astype(jnp.bfloat16)
    width = 256
    page_row = lax.broadcasted_iota(jnp.int32, (pages, width), 0)
    token = lax.broadcasted_iota(jnp.int32, (pages, width), 1)
    inside = (lax.broadcasted_iota(jnp.int32, (ROWS, width), 1) % PAGE).astype(jnp.float32)
    for j in range(pages * PAGE // width):
        spread = jnp.where((token + j * width) // PAGE == page_row, 1.0, 0.0).astype(jnp.bfloat16)
        most = jnp.dot(limit, spread, preferred_element_type=jnp.float32)[:ROWS]
        bias_ref[:, j * width : (j + 1) * width] = jnp.where(inside < most, 0.0, HIDDEN)
    own_row = lax.broadcasted_iota(jnp.int32, (ROWS, HD), 0)
    own_column = lax.broadcasted_iota(jnp.int32, (ROWS, HD), 1)
    bias_ref[:, pages * PAGE :] = jnp.where(own_row == own_column, 0.0, HIDDEN)


def parting():
    row = lax.broadcasted_iota(jnp.int32, (256, 256), 0)
    column = lax.broadcasted_iota(jnp.int32, (256, 256), 1)
    source = jnp.where(row < 128, 2 * row, 2 * row - 255)
    return jnp.where(column == source, 1.0, 0.0).astype(jnp.bfloat16)


def attend(stream, queries, keys_ref, values_ref, bias_ref, scores_ref, tokens):
    norm = stream * lax.rsqrt(jnp.mean(stream * stream, axis=1, keepdims=True) + EPS)
    query = (queries + norm).astype(jnp.bfloat16)
    count = GROUP * ROWS
    chunks = [(at, 256) for at in range(0, tokens, 256)] + [(tokens, HD)]
    top = jnp.full((count, HD), HIDDEN, jnp.float32)
    for at, size in chunks:
        part = contract_last(query, keys_ref[at : at + size, :])
        part = part.reshape(GROUP, ROWS, size) + bias_ref[:, at : at + size][None]
        part = part.reshape(count, size)
        scores_ref[:, at : at + size] = part
        for lane in range(0, size, HD):
            top = jnp.maximum(top, part[:, lane : lane + HD])
    top = jnp.max(top, axis=1, keepdims=True) * EXP2_SCALE
    total = jnp.zeros((count, HD), jnp.float32)
    mixed = jnp.zeros((count, HD), jnp.float32)
    for at, size in chunks:
        part = jnp.exp2(scores_ref[:, at : at + size] * EXP2_SCALE - top)
        for lane in range(0, size, HD):
            total = total + part[:, lane : lane + HD]
        mixed = mixed + jnp.dot(
            part.astype(jnp.bfloat16),
            values_ref[at : at + size, :],
            preferred_element_type=jnp.float32,
        )
    attended = (mixed / jnp.sum(total, axis=1, keepdims=True)).astype(jnp.bfloat16)
    return attended, (stream + attended.astype(jnp.float32)).astype(jnp.bfloat16)


def relay(
    sections,
    pages,
    kv_ref,
    queries_ref,
    new_ref,
    stream_ref,
    page_map_ref,
    counts_ref,
    fill_ref,
    out_ref,
    keys_ref,
    values_ref,
    bias_ref,
    scores_ref,
    arrived,
    leaving,
    send_sem,
    recv_sem,
):
    me = lax.axis_index("section")
    after, before = lax.rem(me + 1, sections), lax.rem(me + sections - 1, sections)
    barrier = pltpu.get_barrier_semaphore()
    for neighbour in (before, after):
        pl.semaphore_signal(barrier, inc=1, device_id={"section": neighbour}, device_id_type=MESH)
    pl.semaphore_wait(barrier, 2)
    tokens = pages * PAGE
    build_bias(page_map_ref, counts_ref, fill_ref, bias_ref, pages)
    part = parting()
    for c in range(tokens // 128):
        both = jnp.dot(part, kv_ref[c * 256 : (c + 1) * 256, :], preferred_element_type=jnp.float32)
        keys_ref[c * 128 : (c + 1) * 128, :] = both[:128].astype(jnp.bfloat16)
        values_ref[c * 128 : (c + 1) * 128, :] = both[128:].astype(jnp.bfloat16)
    new = new_ref[...].astype(jnp.float32)
    blank = jnp.zeros((HD - ROWS, HD), jnp.float32)
    keys_ref[tokens:, :] = jnp.concatenate([new[:, :HD], blank], 0).astype(jnp.bfloat16)
    values_ref[tokens:, :] = jnp.concatenate([new[:, HD:], blank], 0).astype(jnp.bfloat16)
    copy = pltpu.make_async_remote_copy(
        src_ref=leaving,
        dst_ref=arrived,
        send_sem=send_sem,
        recv_sem=recv_sem,
        device_id={"section": after},
        device_id_type=MESH,
    )

    @pl.when(me == 0)
    def _():
        arrived[...] = by_group(stream_ref[...]).astype(jnp.bfloat16)

    @pl.when(me > 0)
    def _():
        copy.wait_recv()

    attended, passed = attend(
        arrived[...].astype(jnp.float32),
        by_group(queries_ref[...]),
        keys_ref,
        values_ref,
        bias_ref,
        scores_ref,
        tokens,
    )
    leaving[...] = passed

    @pl.when(me < sections - 1)
    def _():
        copy.start()

    out_ref[...] = attended

    @pl.when(me < sections - 1)
    def _():
        copy.wait_send()


def shards(pool, queries, new_kv, stream_in, page_map, page_counts, last_fill):
    sections = lax.axis_size("section")
    pages = page_map.shape[0]
    tokens = pages * PAGE
    arrived = lax.all_to_all(pool, ("section", "tp"), split_axis=1, concat_axis=0, tiled=True)
    kv = arrived.reshape(pages, 2, PAGE, HD).transpose(0, 2, 1, 3).reshape(pages * 2 * PAGE, HD)
    vmem = pl.BlockSpec(memory_space=pltpu.VMEM)
    smem = pl.BlockSpec(memory_space=pltpu.SMEM)
    out = pl.pallas_call(
        lambda *refs: relay(sections, pages, *refs),
        out_shape=jax.ShapeDtypeStruct((GROUP * ROWS, HD), jnp.bfloat16),
        in_specs=[vmem] * 5 + [smem] * 2,
        out_specs=vmem,
        scratch_shapes=[
            pltpu.VMEM((tokens + HD, HD), jnp.bfloat16),
            pltpu.VMEM((tokens + HD, HD), jnp.bfloat16),
            pltpu.VMEM((ROWS, tokens + HD), jnp.float32),
            pltpu.VMEM((GROUP * ROWS, tokens + HD), jnp.float32),
            pltpu.VMEM((GROUP * ROWS, HD), jnp.bfloat16),
            pltpu.VMEM((GROUP * ROWS, HD), jnp.bfloat16),
            pltpu.SemaphoreType.DMA,
            pltpu.SemaphoreType.DMA,
        ],
        compiler_params=pltpu.CompilerParams(
            collective_id=0, has_side_effects=True, vmem_limit_bytes=32 * 1024 * 1024
        ),
    )(
        kv,
        queries[0],
        new_kv.reshape(ROWS, 2 * HD),
        stream_in,
        page_map.reshape(1, pages),
        page_counts,
        last_fill,
    )
    return out.reshape(GROUP, ROWS, HD).transpose(1, 0, 2).reshape(1, ROWS, GROUP * HD)


def solution(mesh):
    in_specs = (
        P(("rep", "section", "tp"), None, None, None),
        P("section", "rep", "tp"),
        P("section", "rep", None, "tp"),
        P("rep", "tp"),
        P("rep"),
        P("rep"),
        P("rep"),
    )
    out_specs = P("section", "rep", "tp")
    return jax.shard_map(shards, mesh=mesh, in_specs=in_specs, out_specs=out_specs, check_vma=False)
```

```python
import math

import jax
import jax.numpy as jnp
from jax import lax
from jax.experimental import pallas as pl
from jax.experimental.pallas import tpu as pltpu
from jax.sharding import PartitionSpec as P

HD = 128
PAGE = 16
GROUP = 16
ROWS = 8
EPS = 1e-05
HIDDEN = -1e30
SEGMENTS = 4
FIRST_HOST = 5
AHEAD = 2
BUNDLE = 2
FAR_AFTER = 1
MESH = pl.DeviceIdType.MESH
EXP2_SCALE = math.log2(math.e) / math.sqrt(HD)


def contract_last(a, b):
    return lax.dot_general(a, b, (((1,), (1,)), ((), ())), preferred_element_type=jnp.float32)


def by_group(block):
    wide = block.astype(jnp.float32)
    return jnp.concatenate([wide[:, g * HD : (g + 1) * HD] for g in range(GROUP)], axis=0)


def build_bias(page_map_ref, counts_ref, fill_ref, bias_ref, pages):
    place = lax.broadcasted_iota(jnp.int32, (16, pages), 1)
    row = lax.broadcasted_iota(jnp.int32, (16, pages), 0)
    limit = jnp.zeros((16, pages), jnp.int32)
    first = jnp.int32(0)
    for r in range(ROWS):
        last = first + counts_ref[r] - 1
        here = jnp.where(place < last, PAGE, jnp.where(place == last, fill_ref[r], 0))
        here = jnp.where(place >= first, here, 0)
        limit = jnp.where(row == r, here, limit)
        first = last + 1
    owner = page_map_ref[...] == lax.broadcasted_iota(jnp.int32, (pages, pages), 0)
    limit = contract_last(
        limit.astype(jnp.float32).astype(jnp.bfloat16),
        jnp.where(owner, 1.0, 0.0).astype(jnp.bfloat16),
    ).astype(jnp.bfloat16)
    width = 256
    page_row = lax.broadcasted_iota(jnp.int32, (pages, width), 0)
    token = lax.broadcasted_iota(jnp.int32, (pages, width), 1)
    inside = (lax.broadcasted_iota(jnp.int32, (ROWS, width), 1) % PAGE).astype(jnp.float32)
    for j in range(pages * PAGE // width):
        spread = jnp.where((token + j * width) // PAGE == page_row, 1.0, 0.0).astype(jnp.bfloat16)
        most = jnp.dot(limit, spread, preferred_element_type=jnp.float32)[:ROWS]
        bias_ref[:, j * width : (j + 1) * width] = jnp.where(inside < most, 0.0, HIDDEN)
    own_row = lax.broadcasted_iota(jnp.int32, (ROWS, HD), 0)
    own_column = lax.broadcasted_iota(jnp.int32, (ROWS, HD), 1)
    bias_ref[:, pages * PAGE :] = jnp.where(own_row == own_column, 0.0, HIDDEN)


def parting():
    row = lax.broadcasted_iota(jnp.int32, (256, 256), 0)
    column = lax.broadcasted_iota(jnp.int32, (256, 256), 1)
    source = jnp.where(row < 128, 2 * row, 2 * row - 255)
    return jnp.where(column == source, 1.0, 0.0).astype(jnp.bfloat16)


def attend(stream, queries, keys_ref, values_ref, bias_ref, scores_ref, tokens):
    norm = stream * lax.rsqrt(jnp.mean(stream * stream, axis=1, keepdims=True) + EPS)
    query = (queries + norm).astype(jnp.bfloat16)
    count = GROUP * ROWS
    chunks = [(at, 256) for at in range(0, tokens, 256)] + [(tokens, HD)]
    top = jnp.full((count, HD), HIDDEN, jnp.float32)
    for at, size in chunks:
        part = contract_last(query, keys_ref[at : at + size, :])
        part = part.reshape(GROUP, ROWS, size) + bias_ref[:, at : at + size][None]
        part = part.reshape(count, size)
        scores_ref[:, at : at + size] = part
        for lane in range(0, size, HD):
            top = jnp.maximum(top, part[:, lane : lane + HD])
    top = jnp.max(top, axis=1, keepdims=True) * EXP2_SCALE
    total = jnp.zeros((count, HD), jnp.float32)
    mixed = jnp.zeros((count, HD), jnp.float32)
    for at, size in chunks:
        part = jnp.exp2(scores_ref[:, at : at + size] * EXP2_SCALE - top)
        for lane in range(0, size, HD):
            total = total + part[:, lane : lane + HD]
        mixed = mixed + jnp.dot(
            part.astype(jnp.bfloat16),
            values_ref[at : at + size, :],
            preferred_element_type=jnp.float32,
        )
    attended = (mixed / jnp.sum(total, axis=1, keepdims=True)).astype(jnp.bfloat16)
    return attended, (stream + attended.astype(jnp.float32)).astype(jnp.bfloat16)


def host_of(sections, segments, tp, segment):
    apart = sections // (2 * segments)
    return lax.rem(apart * segment + FIRST_HOST + lax.rem(tp, 2) * (sections // 2), sections)


def fused(
    sections,
    heads,
    pool_ref,
    queries_ref,
    new_ref,
    stream_ref,
    page_map_ref,
    counts_ref,
    fill_ref,
    out_ref,
    row_ref,
    pages_ref,
    keys_ref,
    values_ref,
    bias_ref,
    scores_ref,
    asked,
    asking,
    arrived,
    leaving,
    results,
    row_send,
    row_recv,
    page_send,
    page_recv,
    ask_send,
    ask_recv,
    stream_send,
    stream_recv,
    out_send,
    out_recv,
    far_sem,
):
    z, tp = lax.axis_index("section"), lax.axis_index("tp")
    depth = pages_ref.shape[0]
    segments = sections // depth
    pages = sections * heads
    tokens = pages * PAGE
    count = GROUP * ROWS

    def at_section(other):
        return {"section": other}

    def push(src, dst, send_sem, recv_sem, other):
        @pl.when(other == z)
        def _():
            pltpu.make_async_copy(src, dst, recv_sem).start()

        @pl.when(other != z)
        def _():
            pltpu.make_async_remote_copy(
                src_ref=src,
                dst_ref=dst,
                send_sem=send_sem,
                recv_sem=recv_sem,
                device_id=at_section(other),
                device_id_type=MESH,
            ).start()

    def wait_bytes(ref, sem):
        pltpu.make_async_copy(ref, ref, sem).wait()

    segment = jnp.int32(-1)
    for s in range(segments):
        segment = jnp.where(host_of(sections, segments, tp, s) == z, s, segment)
    hosting = segment >= 0

    reach = sections // 4
    barrier = pltpu.get_barrier_semaphore()
    for d in range(1, reach + 1):
        for other in (lax.rem(z + d, sections), lax.rem(z + sections - d, sections)):
            pl.semaphore_signal(
                barrier, inc=1, device_id=at_section(other), device_id_type=MESH
            )
    for d in range(1, heads):
        pl.semaphore_signal(
            barrier, inc=1, device_id={"tp": lax.rem(tp + d, heads)}, device_id_type=MESH
        )
    asking[:count, :] = by_group(queries_ref[...]).astype(jnp.bfloat16)
    new = new_ref[...].astype(jnp.float32)
    asking[count:, :] = jnp.concatenate([new[:, :HD], new[:, HD:]], 0).astype(jnp.bfloat16)
    pl.semaphore_wait(barrier, heads - 1 + 2 * reach)
    for other in (lax.rem(z + reach, sections), lax.rem(z + sections - reach, sections)):
        pl.semaphore_signal(far_sem, inc=1, device_id=at_section(other), device_id_type=MESH)

    bundles = sections // BUNDLE
    for b in range(bundles):
        layers = pl.ds(b * BUNDLE, BUNDLE)
        for d in range(1, heads):
            other = lax.rem(tp + d, heads)
            pltpu.make_async_remote_copy(
                src_ref=pool_ref.at[layers, other],
                dst_ref=row_ref.at[layers, tp],
                send_sem=row_send,
                recv_sem=row_recv.at[b],
                device_id={"tp": other},
                device_id_type=MESH,
            ).start()
        pltpu.make_async_copy(
            pool_ref.at[layers, tp], row_ref.at[layers, tp], row_recv.at[b]
        ).start()

    def forward(b, near):
        s = b * BUNDLE // depth
        host = host_of(sections, segments, tp, s)
        ahead = lax.rem(host - z + sections, sections)
        close = jnp.logical_or(ahead <= reach, ahead >= sections - reach)

        @pl.when(close if near else jnp.logical_not(close))
        def _():
            for i in range(BUNDLE):
                j = (b * BUNDLE + i) % depth
                push(row_ref.at[s * depth + j], pages_ref.at[j, z], page_send, page_recv.at[j], host)

    for b in range(bundles):
        wait_bytes(row_ref.at[pl.ds(b * BUNDLE, BUNDLE)], row_recv.at[b])
        forward(b, True)
        if b == FAR_AFTER:
            pl.semaphore_wait(far_sem, 2)
            push(asking, asked.at[lax.rem(z, depth)], ask_send, ask_recv,
                 host_of(sections, segments, tp, z // depth))
            for earlier in range(b):
                forward(earlier, False)
        if b >= FAR_AFTER:
            forward(b, False)

    @pl.when(hosting)
    def _():
        build_bias(page_map_ref, counts_ref, fill_ref, bias_ref, pages)
        wait_bytes(asked, ask_recv)
        part = parting()
        blank = jnp.zeros((HD - ROWS, HD), jnp.float32)

        def prepare(j):
            wait_bytes(pages_ref.at[j], page_recv.at[j])
            for c in range(tokens // 128):
                per = 256 // (2 * PAGE * heads)
                mixed = pages_ref[j, c * per : (c + 1) * per].reshape(256, HD)
                both = jnp.dot(part, mixed, preferred_element_type=jnp.float32)
                keys_ref[j, c * 128 : (c + 1) * 128, :] = both[:128].astype(jnp.bfloat16)
                values_ref[j, c * 128 : (c + 1) * 128, :] = both[128:].astype(jnp.bfloat16)
            new = asked[j, count:, :].astype(jnp.float32)
            keys_ref[j, tokens:, :] = jnp.concatenate([new[:ROWS], blank], 0).astype(jnp.bfloat16)
            values_ref[j, tokens:, :] = jnp.concatenate([new[ROWS:], blank], 0).astype(jnp.bfloat16)

        def run(j):
            attended, passed = attend(
                arrived[...].astype(jnp.float32),
                asked[j, :count, :].astype(jnp.float32),
                keys_ref.at[j],
                values_ref.at[j],
                bias_ref,
                scores_ref,
                tokens,
            )
            results[j] = attended
            push(results.at[j], out_ref, out_send, out_recv, segment * depth + j)
            return passed

        for j in range(AHEAD):
            prepare(j)

        onward = pltpu.make_async_remote_copy(
            src_ref=leaving,
            dst_ref=arrived,
            send_sem=stream_send,
            recv_sem=stream_recv,
            device_id=at_section(host_of(sections, segments, tp, lax.rem(segment + 1, segments))),
            device_id_type=MESH,
        )

        @pl.when(segment == 0)
        def _():
            arrived[...] = by_group(stream_ref[...]).astype(jnp.bfloat16)

        @pl.when(segment > 0)
        def _():
            onward.wait_recv()

        for j in range(depth):
            if j >= AHEAD:
                prepare(j)
            passed = run(j)
            if j < depth - 1:
                arrived[...] = passed
            else:
                leaving[...] = passed

        @pl.when(segment < segments - 1)
        def _():
            onward.start()

    wait_bytes(out_ref, out_recv)
    sent = row_ref.at[:, pl.ds(0, heads - 1)]
    wait_bytes(sent, row_send)

    @pl.when(host_of(sections, segments, tp, z // depth) != z)
    def _():
        wait_bytes(asking, ask_send)

    @pl.when(hosting)
    def _():
        wait_bytes(row_ref.at[pl.ds(0, sections - depth)], page_send)
        at_home = z // depth == segment

        @pl.when(at_home)
        def _():
            wait_bytes(results.at[pl.ds(0, depth - 1)], out_send)

        @pl.when(jnp.logical_not(at_home))
        def _():
            wait_bytes(results, out_send)

        @pl.when(segment < segments - 1)
        def _():
            wait_bytes(leaving, stream_send)

    @pl.when(jnp.logical_not(hosting))
    def _():
        wait_bytes(row_ref, page_send)


def shards(pool, queries, new_kv, stream_in, page_map, page_counts, last_fill):
    sections, heads = lax.axis_size("section"), lax.axis_size("tp")
    pages = page_map.shape[0]
    tokens = pages * PAGE
    depth = max(2, sections // SEGMENTS)
    count = GROUP * ROWS
    slots = pool.reshape(sections, heads, 2, PAGE, HD).transpose(0, 1, 3, 2, 4)
    slots = slots.reshape(sections, heads, 2 * PAGE, HD)
    vmem = pl.BlockSpec(memory_space=pltpu.VMEM)
    smem = pl.BlockSpec(memory_space=pltpu.SMEM)
    dma = pltpu.SemaphoreType.DMA
    half = jnp.bfloat16
    out = pl.pallas_call(
        lambda *refs: fused(sections, heads, *refs),
        out_shape=jax.ShapeDtypeStruct((count, HD), half),
        in_specs=[pl.BlockSpec(memory_space=pl.ANY)] + [vmem] * 4 + [smem] * 2,
        out_specs=vmem,
        scratch_shapes=[
            pltpu.VMEM((sections, heads, 2 * PAGE, HD), half),
            pltpu.VMEM((depth, sections, heads, 2 * PAGE, HD), half),
            pltpu.VMEM((depth, tokens + HD, HD), half),
            pltpu.VMEM((depth, tokens + HD, HD), half),
            pltpu.VMEM((ROWS, tokens + HD), jnp.float32),
            pltpu.VMEM((count, tokens + HD), jnp.float32),
            pltpu.VMEM((depth, count + 2 * ROWS, HD), half),
            pltpu.VMEM((count + 2 * ROWS, HD), half),
            pltpu.VMEM((count, HD), half),
            pltpu.VMEM((count, HD), half),
            pltpu.VMEM((depth, count, HD), half),
            dma,
            dma((sections // BUNDLE,)),
            dma,
            dma((depth,)),
            dma,
            dma,
            dma,
            dma,
            dma,
            dma,
            pltpu.SemaphoreType.REGULAR,
        ],
        compiler_params=pltpu.CompilerParams(
            collective_id=0, has_side_effects=True, vmem_limit_bytes=32 * 1024 * 1024
        ),
    )(
        slots,
        queries[0],
        new_kv.reshape(ROWS, 2 * HD),
        stream_in,
        page_map.reshape(1, pages),
        page_counts,
        last_fill,
    )
    return out.reshape(GROUP, ROWS, HD).transpose(1, 0, 2).reshape(1, ROWS, GROUP * HD)


def solution(mesh):
    in_specs = (
        P(("rep", "section", "tp"), None, None, None),
        P("section", "rep", "tp"),
        P("section", "rep", None, "tp"),
        P("rep", "tp"),
        P("rep"),
        P("rep"),
        P("rep"),
    )
    out_specs = P("section", "rep", "tp")
    return jax.shard_map(shards, mesh=mesh, in_specs=in_specs, out_specs=out_specs, check_vma=False)
```

```python
import math

import jax
import jax.numpy as jnp
from jax import lax
from jax.experimental import pallas as pl
from jax.experimental.pallas import tpu as pltpu
from jax.sharding import PartitionSpec as P

HD = 128
PAGE = 16
GROUP = 16
ROWS = 8
EPS = 1e-05
HIDDEN = -1e30
SEGMENTS = 4
FIRST_HOST = 4
AHEAD = 3
NEAR_FIRST = 2
MESH = pl.DeviceIdType.MESH
EXP2_SCALE = math.log2(math.e) / math.sqrt(HD)


def contract_last(a, b):
    return lax.dot_general(a, b, (((1,), (1,)), ((), ())), preferred_element_type=jnp.float32)


def by_group(block):
    wide = block.astype(jnp.float32)
    return jnp.concatenate([wide[:, g * HD : (g + 1) * HD] for g in range(GROUP)], axis=0)


def build_bias(page_map_ref, counts_ref, fill_ref, bias_ref, pages):
    place = lax.broadcasted_iota(jnp.int32, (16, pages), 1)
    row = lax.broadcasted_iota(jnp.int32, (16, pages), 0)
    limit = jnp.zeros((16, pages), jnp.int32)
    first = jnp.int32(0)
    for r in range(ROWS):
        last = first + counts_ref[r] - 1
        here = jnp.where(place < last, PAGE, jnp.where(place == last, fill_ref[r], 0))
        here = jnp.where(place >= first, here, 0)
        limit = jnp.where(row == r, here, limit)
        first = last + 1
    owner = page_map_ref[...] == lax.broadcasted_iota(jnp.int32, (pages, pages), 0)
    limit = contract_last(
        limit.astype(jnp.float32).astype(jnp.bfloat16),
        jnp.where(owner, 1.0, 0.0).astype(jnp.bfloat16),
    ).astype(jnp.bfloat16)
    width = 256
    page_row = lax.broadcasted_iota(jnp.int32, (pages, width), 0)
    token = lax.broadcasted_iota(jnp.int32, (pages, width), 1)
    inside = (lax.broadcasted_iota(jnp.int32, (ROWS, width), 1) % PAGE).astype(jnp.float32)
    for j in range(pages * PAGE // width):
        spread = jnp.where((token + j * width) // PAGE == page_row, 1.0, 0.0).astype(jnp.bfloat16)
        most = jnp.dot(limit, spread, preferred_element_type=jnp.float32)[:ROWS]
        bias_ref[:, j * width : (j + 1) * width] = jnp.where(inside < most, 0.0, HIDDEN)
    own_row = lax.broadcasted_iota(jnp.int32, (ROWS, HD), 0)
    own_column = lax.broadcasted_iota(jnp.int32, (ROWS, HD), 1)
    bias_ref[:, pages * PAGE :] = jnp.where(own_row == own_column, 0.0, HIDDEN)


def parting():
    row = lax.broadcasted_iota(jnp.int32, (256, 256), 0)
    column = lax.broadcasted_iota(jnp.int32, (256, 256), 1)
    source = jnp.where(row < 128, 2 * row, 2 * row - 255)
    return jnp.where(column == source, 1.0, 0.0).astype(jnp.bfloat16)


def attend(stream, queries, keys_ref, values_ref, bias_ref, scores_ref, tokens):
    norm = stream * lax.rsqrt(jnp.mean(stream * stream, axis=1, keepdims=True) + EPS)
    query = (queries + norm).astype(jnp.bfloat16)
    count = GROUP * ROWS
    chunks = [(at, 256) for at in range(0, tokens, 256)] + [(tokens, HD)]
    top = jnp.full((count, HD), HIDDEN, jnp.float32)
    for at, size in chunks:
        part = contract_last(query, keys_ref[at : at + size, :])
        part = part.reshape(GROUP, ROWS, size) + bias_ref[:, at : at + size][None]
        part = part.reshape(count, size)
        scores_ref[:, at : at + size] = part
        for lane in range(0, size, HD):
            top = jnp.maximum(top, part[:, lane : lane + HD])
    top = jnp.max(top, axis=1, keepdims=True) * EXP2_SCALE
    total = jnp.zeros((count, HD), jnp.float32)
    mixed = jnp.zeros((count, HD), jnp.float32)
    for at, size in chunks:
        part = jnp.exp2(scores_ref[:, at : at + size] * EXP2_SCALE - top)
        for lane in range(0, size, HD):
            total = total + part[:, lane : lane + HD]
        mixed = mixed + jnp.dot(
            part.astype(jnp.bfloat16),
            values_ref[at : at + size, :],
            preferred_element_type=jnp.float32,
        )
    attended = (mixed / jnp.sum(total, axis=1, keepdims=True)).astype(jnp.bfloat16)
    return attended, (stream + attended.astype(jnp.float32)).astype(jnp.bfloat16)


def host_of(sections, segments, head, segment):
    apart = sections // (2 * segments)
    start = FIRST_HOST + head // 2 + lax.rem(head, 2) * (sections // 2)
    return lax.rem(apart * segment + start, sections)


def fused(
    sections,
    heads,
    pool_ref,
    queries_ref,
    new_ref,
    stream_ref,
    page_map_ref,
    counts_ref,
    fill_ref,
    out_ref,
    pages_ref,
    keys_ref,
    values_ref,
    bias_ref,
    scores_ref,
    asked,
    asking,
    arrived,
    leaving,
    results,
    page_send,
    page_recv,
    ask_send,
    ask_recv,
    stream_send,
    stream_recv,
    out_send,
    out_recv,
    near_sem,
    far_sem,
    all_sem,
):
    z, tp = lax.axis_index("section"), lax.axis_index("tp")
    depth = pages_ref.shape[0]
    segments = sections // depth
    pages = sections * heads
    tokens = pages * PAGE
    count = GROUP * ROWS

    def at_section(other):
        return {"section": other}

    def push(src, dst, send_sem, recv_sem, other):
        @pl.when(other == z)
        def _():
            pltpu.make_async_copy(src, dst, recv_sem).start()

        @pl.when(other != z)
        def _():
            pltpu.make_async_remote_copy(
                src_ref=src,
                dst_ref=dst,
                send_sem=send_sem,
                recv_sem=recv_sem,
                device_id=at_section(other),
                device_id_type=MESH,
            ).start()

    def wait_bytes(ref, sem):
        pltpu.make_async_copy(ref, ref, sem).wait()

    segment = jnp.int32(-1)
    for s in range(segments):
        segment = jnp.where(host_of(sections, segments, tp, s) == z, s, segment)
    hosting = segment >= 0

    reach = sections // 4
    row_peers = [lax.rem(tp + d, heads) for d in range(1, heads)]

    def tell_row(sem):
        for other in row_peers:
            pl.semaphore_signal(sem, inc=1, device_id={"tp": other}, device_id_type=MESH)

    barrier = pltpu.get_barrier_semaphore()
    for d in range(1, reach + 1):
        for other in (lax.rem(z + d, sections), lax.rem(z + sections - d, sections)):
            pl.semaphore_signal(
                barrier, inc=1, device_id=at_section(other), device_id_type=MESH
            )
    tell_row(barrier)
    asking[:count, :] = by_group(queries_ref[...]).astype(jnp.bfloat16)
    new = new_ref[...].astype(jnp.float32)
    asking[count:, :] = jnp.concatenate([new[:, :HD], new[:, HD:]], 0).astype(jnp.bfloat16)
    pl.semaphore_wait(barrier, heads - 1 + 2 * reach)
    tell_row(near_sem)
    for other in (lax.rem(z + reach, sections), lax.rem(z + sections - reach, sections)):
        pl.semaphore_signal(far_sem, inc=1, device_id=at_section(other), device_id_type=MESH)

    me = z * heads + tp

    def scatter(s, near):
        def step(i, carry):
            j = i // heads
            head = lax.rem(z + tp + i, heads)
            host = host_of(sections, segments, head, s)
            ahead = lax.rem(host - z + sections, sections)
            close = jnp.logical_or(ahead <= reach, ahead >= sections - reach)
            src = pool_ref.at[s * depth + j, head]
            dst = pages_ref.at[j, me]
            mine = jnp.logical_and(host == z, head == tp)
            wanted = close if near else jnp.logical_not(close)
            if near is None:
                wanted = jnp.bool_(True)

            @pl.when(jnp.logical_and(wanted, mine))
            def _():
                pltpu.make_async_copy(src, dst, page_recv.at[j]).start()

            @pl.when(jnp.logical_and(wanted, jnp.logical_not(mine)))
            def _():
                pltpu.make_async_remote_copy(
                    src_ref=src,
                    dst_ref=dst,
                    send_sem=page_send,
                    recv_sem=page_recv.at[j],
                    device_id={"section": host, "tp": head},
                    device_id_type=MESH,
                ).start()

            return carry

        lax.fori_loop(0, depth * heads, step, 0)

    pl.semaphore_wait(near_sem, heads - 1)
    if NEAR_FIRST >= 1:
        scatter(0, True)
    pl.semaphore_wait(far_sem, 2)
    tell_row(all_sem)
    push(asking, asked.at[lax.rem(z, depth)], ask_send, ask_recv,
         host_of(sections, segments, tp, z // depth))
    for s in range(1, NEAR_FIRST):
        scatter(s, True)
    pl.semaphore_wait(all_sem, heads - 1)
    for s in range(segments):
        scatter(s, False if s < NEAR_FIRST else None)

    @pl.when(hosting)
    def _():
        build_bias(page_map_ref, counts_ref, fill_ref, bias_ref, pages)
        wait_bytes(asked, ask_recv)
        part = parting()
        blank = jnp.zeros((HD - ROWS, HD), jnp.float32)

        def prepare(j):
            wait_bytes(pages_ref.at[j], page_recv.at[j])
            for c in range(tokens // 128):
                per = 256 // (2 * PAGE)
                mixed = pages_ref[j, c * per : (c + 1) * per].reshape(256, HD)
                both = jnp.dot(part, mixed, preferred_element_type=jnp.float32)
                keys_ref[j, c * 128 : (c + 1) * 128, :] = both[:128].astype(jnp.bfloat16)
                values_ref[j, c * 128 : (c + 1) * 128, :] = both[128:].astype(jnp.bfloat16)
            new = asked[j, count:, :].astype(jnp.float32)
            keys_ref[j, tokens:, :] = jnp.concatenate([new[:ROWS], blank], 0).astype(jnp.bfloat16)
            values_ref[j, tokens:, :] = jnp.concatenate([new[ROWS:], blank], 0).astype(jnp.bfloat16)

        def run(j):
            attended, passed = attend(
                arrived[...].astype(jnp.float32),
                asked[j, :count, :].astype(jnp.float32),
                keys_ref.at[j],
                values_ref.at[j],
                bias_ref,
                scores_ref,
                tokens,
            )
            results[j] = attended
            push(results.at[j], out_ref, out_send, out_recv, segment * depth + j)
            return passed

        for j in range(AHEAD):
            prepare(j)

        onward = pltpu.make_async_remote_copy(
            src_ref=leaving,
            dst_ref=arrived,
            send_sem=stream_send,
            recv_sem=stream_recv,
            device_id=at_section(host_of(sections, segments, tp, lax.rem(segment + 1, segments))),
            device_id_type=MESH,
        )

        @pl.when(segment == 0)
        def _():
            arrived[...] = by_group(stream_ref[...]).astype(jnp.bfloat16)

        @pl.when(segment > 0)
        def _():
            onward.wait_recv()

        for j in range(depth):
            if j >= AHEAD:
                prepare(j)
            passed = run(j)
            if j < depth - 1:
                arrived[...] = passed
            else:
                leaving[...] = passed

        @pl.when(segment < segments - 1)
        def _():
            onward.start()

    wait_bytes(out_ref, out_recv)

    @pl.when(host_of(sections, segments, tp, z // depth) != z)
    def _():
        wait_bytes(asking, ask_send)

    @pl.when(hosting)
    def _():
        wait_bytes(pool_ref.at[pl.ds(0, sections - 1)], page_send)
        wait_bytes(pool_ref.at[0, pl.ds(0, heads - depth)], page_send)
        at_home = z // depth == segment

        @pl.when(at_home)
        def _():
            wait_bytes(results.at[pl.ds(0, depth - 1)], out_send)

        @pl.when(jnp.logical_not(at_home))
        def _():
            wait_bytes(results, out_send)

        @pl.when(segment < segments - 1)
        def _():
            wait_bytes(leaving, stream_send)

    @pl.when(jnp.logical_not(hosting))
    def _():
        wait_bytes(pool_ref, page_send)


def shards(pool, queries, new_kv, stream_in, page_map, page_counts, last_fill):
    sections, heads = lax.axis_size("section"), lax.axis_size("tp")
    pages = page_map.shape[0]
    tokens = pages * PAGE
    depth = sections // SEGMENTS
    count = GROUP * ROWS
    slots = pool.reshape(sections, heads, 2, PAGE, HD).transpose(0, 1, 3, 2, 4)
    slots = slots.reshape(sections, heads, 2 * PAGE, HD)
    vmem = pl.BlockSpec(memory_space=pltpu.VMEM)
    smem = pl.BlockSpec(memory_space=pltpu.SMEM)
    dma = pltpu.SemaphoreType.DMA
    half = jnp.bfloat16
    out = pl.pallas_call(
        lambda *refs: fused(sections, heads, *refs),
        out_shape=jax.ShapeDtypeStruct((count, HD), half),
        in_specs=[pl.BlockSpec(memory_space=pl.ANY)] + [vmem] * 4 + [smem] * 2,
        out_specs=vmem,
        scratch_shapes=[
            pltpu.VMEM((depth, pages, 2 * PAGE, HD), half),
            pltpu.VMEM((depth, tokens + HD, HD), half),
            pltpu.VMEM((depth, tokens + HD, HD), half),
            pltpu.VMEM((ROWS, tokens + HD), jnp.float32),
            pltpu.VMEM((count, tokens + HD), jnp.float32),
            pltpu.VMEM((depth, count + 2 * ROWS, HD), half),
            pltpu.VMEM((count + 2 * ROWS, HD), half),
            pltpu.VMEM((count, HD), half),
            pltpu.VMEM((count, HD), half),
            pltpu.VMEM((depth, count, HD), half),
            dma,
            dma((depth,)),
            dma,
            dma,
            dma,
            dma,
            dma,
            dma,
            pltpu.SemaphoreType.REGULAR,
            pltpu.SemaphoreType.REGULAR,
            pltpu.SemaphoreType.REGULAR,
        ],
        compiler_params=pltpu.CompilerParams(
            collective_id=0, has_side_effects=True, vmem_limit_bytes=60 * 1024 * 1024
        ),
    )(
        slots,
        queries[0],
        new_kv.reshape(ROWS, 2 * HD),
        stream_in,
        page_map.reshape(1, pages),
        page_counts,
        last_fill,
    )
    return out.reshape(GROUP, ROWS, HD).transpose(1, 0, 2).reshape(1, ROWS, GROUP * HD)


def solution(mesh):
    in_specs = (
        P(("rep", "section", "tp"), None, None, None),
        P("section", "rep", "tp"),
        P("section", "rep", None, "tp"),
        P("rep", "tp"),
        P("rep"),
        P("rep"),
        P("rep"),
    )
    out_specs = P("section", "rep", "tp")
    return jax.shard_map(shards, mesh=mesh, in_specs=in_specs, out_specs=out_specs, check_vma=False)
```

```python
import functools
import math

import jax
import jax.numpy as jnp
from jax import lax
from jax.experimental import pallas as pl
from jax.experimental.pallas import tpu as pltpu
from jax.sharding import PartitionSpec as P

HD = 128
PAGE = 16
GROUP = 16
ROWS = 8
EPS = 1e-05
HIDDEN = -1e30
STARTS = (0, 4, 8, 12, 16)
FIRST_HOST = 0
AHEAD = 3
NEAR_FIRST = 1
MESH = pl.DeviceIdType.MESH
EXP2_SCALE = math.log2(math.e) / math.sqrt(HD)


def contract_last(a, b):
    return lax.dot_general(a, b, (((1,), (1,)), ((), ())), preferred_element_type=jnp.float32)


def by_group(block):
    wide = block.astype(jnp.float32)
    return jnp.concatenate([wide[:, g * HD : (g + 1) * HD] for g in range(GROUP)], axis=0)


def build_bias(page_map_ref, counts_ref, fill_ref, bias_ref, pages):
    place = lax.broadcasted_iota(jnp.int32, (16, pages), 1)
    row = lax.broadcasted_iota(jnp.int32, (16, pages), 0)
    limit = jnp.zeros((16, pages), jnp.int32)
    first = jnp.int32(0)
    for r in range(ROWS):
        last = first + counts_ref[r] - 1
        here = jnp.where(place < last, PAGE, jnp.where(place == last, fill_ref[r], 0))
        here = jnp.where(place >= first, here, 0)
        limit = jnp.where(row == r, here, limit)
        first = last + 1
    owner = page_map_ref[...] == lax.broadcasted_iota(jnp.int32, (pages, pages), 0)
    limit = contract_last(
        limit.astype(jnp.float32).astype(jnp.bfloat16),
        jnp.where(owner, 1.0, 0.0).astype(jnp.bfloat16),
    ).astype(jnp.bfloat16)
    width = 256
    page_row = lax.broadcasted_iota(jnp.int32, (pages, width), 0)
    token = lax.broadcasted_iota(jnp.int32, (pages, width), 1)
    inside = (lax.broadcasted_iota(jnp.int32, (ROWS, width), 1) % PAGE).astype(jnp.float32)
    for j in range(pages * PAGE // width):
        spread = jnp.where((token + j * width) // PAGE == page_row, 1.0, 0.0).astype(jnp.bfloat16)
        most = jnp.dot(limit, spread, preferred_element_type=jnp.float32)[:ROWS]
        bias_ref[:, j * width : (j + 1) * width] = jnp.where(inside < most, 0.0, HIDDEN)
    own_row = lax.broadcasted_iota(jnp.int32, (ROWS, HD), 0)
    own_column = lax.broadcasted_iota(jnp.int32, (ROWS, HD), 1)
    bias_ref[:, pages * PAGE :] = jnp.where(own_row == own_column, 0.0, HIDDEN)


def parting():
    row = lax.broadcasted_iota(jnp.int32, (256, 256), 0)
    column = lax.broadcasted_iota(jnp.int32, (256, 256), 1)
    source = jnp.where(row < 128, 2 * row, 2 * row - 255)
    return jnp.where(column == source, 1.0, 0.0).astype(jnp.bfloat16)


def attend(stream, queries, keys_ref, values_ref, bias_ref, scores_ref, tokens):
    norm = stream * lax.rsqrt(jnp.mean(stream * stream, axis=1, keepdims=True) + EPS)
    query = (queries + norm).astype(jnp.bfloat16)
    count = GROUP * ROWS
    chunks = [(at, 256) for at in range(0, tokens, 256)] + [(tokens, HD)]
    top = jnp.full((count, HD), HIDDEN, jnp.float32)
    for at, size in chunks:
        part = contract_last(query, keys_ref[at : at + size, :])
        part = part.reshape(GROUP, ROWS, size) + bias_ref[:, at : at + size][None]
        part = part.reshape(count, size)
        scores_ref[:, at : at + size] = part
        for lane in range(0, size, HD):
            top = jnp.maximum(top, part[:, lane : lane + HD])
    top = jnp.max(top, axis=1, keepdims=True) * EXP2_SCALE
    total = jnp.zeros((count, HD), jnp.float32)
    mixed = jnp.zeros((count, HD), jnp.float32)
    for at, size in chunks:
        part = jnp.exp2(scores_ref[:, at : at + size] * EXP2_SCALE - top)
        for lane in range(0, size, HD):
            total = total + part[:, lane : lane + HD]
        mixed = mixed + jnp.dot(
            part.astype(jnp.bfloat16),
            values_ref[at : at + size, :],
            preferred_element_type=jnp.float32,
        )
    attended = (mixed / jnp.sum(total, axis=1, keepdims=True)).astype(jnp.bfloat16)
    return attended, (stream + attended.astype(jnp.float32)).astype(jnp.bfloat16)


def host_of(sections, heads, head, segment):
    columns = heads // 2
    x = lax.rem(head + segment, columns)
    z = lax.rem((sections // heads) * head + FIRST_HOST + lax.rem(x, 2), sections)
    return z, 2 * x + lax.rem(segment, 2)


def hosted_at(sections, heads, segments, z, tp):
    columns, stride = heads // 2, sections // heads
    x = tp // 2
    rest = lax.rem(z - FIRST_HOST - lax.rem(x, 2) + 2 * sections, sections)
    head = rest // stride
    segment = lax.rem(x - head + heads, columns)
    found = jnp.logical_and(lax.rem(rest, stride) == 0, segment < segments)
    found = jnp.logical_and(found, lax.rem(segment, 2) == lax.rem(tp, 2))
    return head, jnp.where(found, segment, -1)


def fused(
    sections,
    heads,
    pool_ref,
    queries_ref,
    new_ref,
    stream_ref,
    page_map_ref,
    counts_ref,
    fill_ref,
    out_ref,
    spare_ref,
    pages_ref,
    keys_ref,
    values_ref,
    bias_ref,
    scores_ref,
    asked,
    asking,
    opening,
    arrived,
    results,
    spare_send,
    spare_recv,
    page_send,
    page_recv,
    ask_send,
    ask_recv,
    open_send,
    stream_send,
    stream_recv,
    out_send,
    out_recv,
    near_sem,
    far_sem,
    all_sem,
):
    z, tp = lax.axis_index("section"), lax.axis_index("tp")
    me = z * heads + tp
    partner = tp + 1 - 2 * lax.rem(tp, 2)
    segments = len(STARTS) - 1
    depths = [STARTS[s + 1] - STARTS[s] for s in range(segments)]
    pages = sections * heads
    tokens = pages * PAGE
    count = GROUP * ROWS

    def place(other):
        return {"section": other[0], "tp": other[1]}

    def here(other):
        return jnp.logical_and(other[0] == z, other[1] == tp)

    def push(src, dst, send_sem, recv_sem, other):
        @pl.when(here(other))
        def _():
            pltpu.make_async_copy(src, dst, recv_sem).start()

        @pl.when(jnp.logical_not(here(other)))
        def _():
            pltpu.make_async_remote_copy(
                src_ref=src,
                dst_ref=dst,
                send_sem=send_sem,
                recv_sem=recv_sem,
                device_id=place(other),
                device_id_type=MESH,
            ).start()

    def wait_bytes(ref, sem):
        pltpu.make_async_copy(ref, ref, sem).wait()

    host = functools.partial(host_of, sections, heads)
    head, segment = hosted_at(sections, heads, segments, z, tp)
    other_segment = hosted_at(sections, heads, segments, z, partner)[1]
    hosting, helping = segment >= 0, other_segment >= 0
    start, depth = jnp.int32(0), jnp.int32(0)
    home_start, home_segment = jnp.int32(0), jnp.int32(0)
    for s in range(segments):
        start = jnp.where(segment == s, STARTS[s], start)
        depth = jnp.where(segment == s, depths[s], depth)
        home_start = jnp.where(z >= STARTS[s], STARTS[s], home_start)
        home_segment = jnp.where(z >= STARTS[s], s, home_segment)
    home_host, first_host = host(tp, home_segment), host(tp, 0)
    opens = z == first_host[0]

    reach = sections // 4

    def tell_row(sem):
        for d in range(1, heads):
            pl.semaphore_signal(
                sem, inc=1, device_id={"tp": lax.rem(tp + d, heads)}, device_id_type=MESH
            )

    barrier = pltpu.get_barrier_semaphore()
    for d in range(1, reach + 1):
        for other in (lax.rem(z + d, sections), lax.rem(z + sections - d, sections)):
            pl.semaphore_signal(
                barrier, inc=1, device_id={"section": other}, device_id_type=MESH
            )
    tell_row(barrier)
    opening[...] = by_group(stream_ref[...]).astype(jnp.bfloat16)
    asking[:count, :] = by_group(queries_ref[...]).astype(jnp.bfloat16)
    new = new_ref[...].astype(jnp.float32)
    asking[count:, :] = jnp.concatenate([new[:, :HD], new[:, HD:]], 0).astype(jnp.bfloat16)
    pl.semaphore_wait(barrier, heads - 1 + 2 * reach)
    tell_row(near_sem)
    for other in (lax.rem(z + reach, sections), lax.rem(z + sections - reach, sections)):
        pl.semaphore_signal(far_sem, inc=1, device_id={"section": other}, device_id_type=MESH)

    def spare(s):
        layers = pl.ds(STARTS[s], depths[s])
        return pltpu.make_async_remote_copy(
            src_ref=pool_ref.at[layers],
            dst_ref=spare_ref.at[layers],
            send_sem=spare_send.at[s],
            recv_sem=spare_recv.at[s],
            device_id={"tp": partner},
            device_id_type=MESH,
        )

    @pl.when(hosting)
    def _():
        for s in range(segments):
            spare(s).start()
            for j in range(depths[s]):

                @pl.when(segment == s)
                def _():
                    pltpu.make_async_copy(
                        pool_ref.at[STARTS[s] + j, head], pages_ref.at[j, me], page_recv.at[j]
                    ).start()

    def scatter(s, near, source_ref, owner):
        def step(i, carry):
            j = i // heads
            goal = lax.rem(z + tp + i, heads)
            other = host(goal, s)
            wanted = jnp.logical_not(jnp.logical_and(other[0] == z, other[1] == owner))
            if near is not None:
                ahead = lax.rem(other[0] - z + sections, sections)
                close = jnp.logical_or(ahead <= reach, ahead >= sections - reach)
                wanted = jnp.logical_and(wanted, close if near else jnp.logical_not(close))

            @pl.when(wanted)
            def _():
                pltpu.make_async_remote_copy(
                    src_ref=source_ref.at[STARTS[s] + j, goal],
                    dst_ref=pages_ref.at[j, z * heads + owner],
                    send_sem=page_send,
                    recv_sem=page_recv.at[j],
                    device_id=place(other),
                    device_id_type=MESH,
                ).start()

            return carry

        lax.fori_loop(0, depths[s] * heads, step, 0)

    pl.semaphore_wait(near_sem, heads - 1)
    pl.semaphore_wait(far_sem, 2)
    tell_row(all_sem)

    @pl.when(jnp.logical_not(hosting))
    def _():
        for s in range(NEAR_FIRST):
            scatter(s, True, pool_ref, tp)

    pl.semaphore_wait(all_sem, heads - 1)
    push(asking, asked.at[z - home_start], ask_send, ask_recv.at[z - home_start], home_host)

    @pl.when(opens)
    def _():
        push(opening, arrived, open_send, stream_recv, first_host)


    @pl.when(jnp.logical_not(hosting))
    def _():
        for s in range(segments):
            scatter(s, False if s < NEAR_FIRST else None, pool_ref, tp)

            @pl.when(helping)
            def _():
                spare(s).wait_recv()
                scatter(s, None, spare_ref, partner)

    @pl.when(hosting)
    def _():
        build_bias(page_map_ref, counts_ref, fill_ref, bias_ref, pages)
        part = parting()
        blank = jnp.zeros((HD - ROWS, HD), jnp.float32)

        def prepare(j):
            wait_bytes(asked.at[j], ask_recv.at[j])
            wait_bytes(pages_ref.at[j], page_recv.at[j])
            for c in range(tokens // 128):
                per = 256 // (2 * PAGE)
                mixed = pages_ref[j, c * per : (c + 1) * per].reshape(256, HD)
                both = jnp.dot(part, mixed, preferred_element_type=jnp.float32)
                keys_ref[j, c * 128 : (c + 1) * 128, :] = both[:128].astype(jnp.bfloat16)
                values_ref[j, c * 128 : (c + 1) * 128, :] = both[128:].astype(jnp.bfloat16)
            new = asked[j, count:, :].astype(jnp.float32)
            keys_ref[j, tokens:, :] = jnp.concatenate([new[:ROWS], blank], 0).astype(jnp.bfloat16)
            values_ref[j, tokens:, :] = jnp.concatenate([new[ROWS:], blank], 0).astype(jnp.bfloat16)

        def run(j):
            attended, passed = attend(
                arrived[...].astype(jnp.float32),
                asked[j, :count, :].astype(jnp.float32),
                keys_ref.at[j],
                values_ref.at[j],
                bias_ref,
                scores_ref,
                tokens,
            )
            arrived[...] = passed
            results[j] = attended

        def deliver(j):
            push(results.at[j], out_ref, out_send.at[j], out_recv, (start + j, head))

        def where_deep(j, act):
            if j < min(depths):
                act(j)
            else:
                pl.when(depth > j)(functools.partial(act, j))

        for j in range(min(AHEAD, max(depths))):
            where_deep(j, prepare)

        onward = pltpu.make_async_remote_copy(
            src_ref=arrived,
            dst_ref=arrived,
            send_sem=stream_send,
            recv_sem=stream_recv,
            device_id=place(host(head, jnp.minimum(segment + 1, segments - 1))),
            device_id_type=MESH,
        )

        onward.wait_recv()

        def advance(j):
            if j >= AHEAD:
                prepare(j)
            run(j)

            @pl.when(jnp.logical_and(j == depth - 1, segment < segments - 1))
            def _():
                onward.start()

            deliver(j)

        for j in range(max(depths)):
            where_deep(j, advance)

        def drain(j):
            @pl.when(jnp.logical_not(here((start + j, head))))
            def _():
                wait_bytes(results.at[j], out_send.at[j])

        for j in range(max(depths)):
            where_deep(j, drain)

        @pl.when(segment < segments - 1)
        def _():
            wait_bytes(arrived, stream_send)

        for s in range(segments):
            spare(s).wait_send()

    wait_bytes(out_ref, out_recv)

    @pl.when(jnp.logical_not(here(home_host)))
    def _():
        wait_bytes(asking, ask_send)

    @pl.when(jnp.logical_and(opens, jnp.logical_not(here(first_host))))
    def _():
        wait_bytes(opening, open_send)

    @pl.when(jnp.logical_not(hosting))
    def _():
        wait_bytes(pool_ref, page_send)

        @pl.when(helping)
        def _():
            wait_bytes(pool_ref.at[pl.ds(0, sections - 1)], page_send)
            for s in range(segments):

                @pl.when(other_segment == s)
                def _():
                    wait_bytes(pool_ref.at[0, pl.ds(0, heads - depths[s])], page_send)


def shards(pool, queries, new_kv, stream_in, page_map, page_counts, last_fill):
    sections, heads = lax.axis_size("section"), lax.axis_size("tp")
    pages = page_map.shape[0]
    tokens = pages * PAGE
    segments = len(STARTS) - 1
    depth = max(STARTS[s + 1] - STARTS[s] for s in range(segments))
    count = GROUP * ROWS
    slots = pool.reshape(sections, heads, 2, PAGE, HD).transpose(0, 1, 3, 2, 4)
    slots = slots.reshape(sections, heads, 2 * PAGE, HD)
    vmem = pl.BlockSpec(memory_space=pltpu.VMEM)
    smem = pl.BlockSpec(memory_space=pltpu.SMEM)
    dma = pltpu.SemaphoreType.DMA
    half = jnp.bfloat16
    out = pl.pallas_call(
        lambda *refs: fused(sections, heads, *refs),
        out_shape=jax.ShapeDtypeStruct((count, HD), half),
        in_specs=[pl.BlockSpec(memory_space=pl.ANY)] + [vmem] * 4 + [smem] * 2,
        out_specs=vmem,
        scratch_shapes=[
            pltpu.VMEM((sections, heads, 2 * PAGE, HD), half),
            pltpu.VMEM((depth, pages, 2 * PAGE, HD), half),
            pltpu.VMEM((depth, tokens + HD, HD), half),
            pltpu.VMEM((depth, tokens + HD, HD), half),
            pltpu.VMEM((ROWS, tokens + HD), jnp.float32),
            pltpu.VMEM((count, tokens + HD), jnp.float32),
            pltpu.VMEM((depth, count + 2 * ROWS, HD), half),
            pltpu.VMEM((count + 2 * ROWS, HD), half),
            pltpu.VMEM((count, HD), half),
            pltpu.VMEM((count, HD), half),
            pltpu.VMEM((depth, count, HD), half),
            dma((segments,)),
            dma((segments,)),
            dma,
            dma((depth,)),
            dma,
            dma((depth,)),
            dma,
            dma,
            dma,
            dma((depth,)),
            dma,
            pltpu.SemaphoreType.REGULAR,
            pltpu.SemaphoreType.REGULAR,
            pltpu.SemaphoreType.REGULAR,
        ],
        compiler_params=pltpu.CompilerParams(
            collective_id=0, has_side_effects=True, vmem_limit_bytes=60 * 1024 * 1024
        ),
    )(
        slots,
        queries[0],
        new_kv.reshape(ROWS, 2 * HD),
        stream_in,
        page_map.reshape(1, pages),
        page_counts,
        last_fill,
    )
    return out.reshape(GROUP, ROWS, HD).transpose(1, 0, 2).reshape(1, ROWS, GROUP * HD)


def solution(mesh):
    in_specs = (
        P(("rep", "section", "tp"), None, None, None),
        P("section", "rep", "tp"),
        P("section", "rep", None, "tp"),
        P("rep", "tp"),
        P("rep"),
        P("rep"),
        P("rep"),
    )
    out_specs = P("section", "rep", "tp")
    return jax.shard_map(shards, mesh=mesh, in_specs=in_specs, out_specs=out_specs, check_vma=False)
```

```python
import functools
import math

import jax
import jax.numpy as jnp
from jax import lax
from jax.experimental import pallas as pl
from jax.experimental.pallas import tpu as pltpu
from jax.sharding import PartitionSpec as P

HD = 128
PAGE = 16
GROUP = 16
ROWS = 8
EPS = 1e-05
HIDDEN = -1e30
STARTS = (0, 4, 8, 12, 16)
FIRST_HOST = 8
AHEAD = 3
NEAR_FIRST = 1
MESH = pl.DeviceIdType.MESH
EXP2_SCALE = math.log2(math.e) / math.sqrt(HD)


def contract_last(a, b):
    return lax.dot_general(a, b, (((1,), (1,)), ((), ())), preferred_element_type=jnp.float32)


def by_group(block):
    wide = block.astype(jnp.float32)
    return jnp.concatenate([wide[:, g * HD : (g + 1) * HD] for g in range(GROUP)], axis=0)


def build_bias(page_map_ref, counts_ref, fill_ref, bias_ref, pages):
    place = lax.broadcasted_iota(jnp.int32, (16, pages), 1)
    row = lax.broadcasted_iota(jnp.int32, (16, pages), 0)
    limit = jnp.zeros((16, pages), jnp.int32)
    first = jnp.int32(0)
    for r in range(ROWS):
        last = first + counts_ref[r] - 1
        here = jnp.where(place < last, PAGE, jnp.where(place == last, fill_ref[r], 0))
        here = jnp.where(place >= first, here, 0)
        limit = jnp.where(row == r, here, limit)
        first = last + 1
    owner = page_map_ref[...] == lax.broadcasted_iota(jnp.int32, (pages, pages), 0)
    limit = contract_last(
        limit.astype(jnp.float32).astype(jnp.bfloat16),
        jnp.where(owner, 1.0, 0.0).astype(jnp.bfloat16),
    ).astype(jnp.bfloat16)
    width = 256
    page_row = lax.broadcasted_iota(jnp.int32, (pages, width), 0)
    token = lax.broadcasted_iota(jnp.int32, (pages, width), 1)
    inside = (lax.broadcasted_iota(jnp.int32, (ROWS, width), 1) % PAGE).astype(jnp.float32)
    for j in range(pages * PAGE // width):
        spread = jnp.where((token + j * width) // PAGE == page_row, 1.0, 0.0).astype(jnp.bfloat16)
        most = jnp.dot(limit, spread, preferred_element_type=jnp.float32)[:ROWS]
        bias_ref[:, j * width : (j + 1) * width] = jnp.where(inside < most, 0.0, HIDDEN)
    own_row = lax.broadcasted_iota(jnp.int32, (ROWS, HD), 0)
    own_column = lax.broadcasted_iota(jnp.int32, (ROWS, HD), 1)
    bias_ref[:, pages * PAGE :] = jnp.where(own_row == own_column, 0.0, HIDDEN)


def parting():
    row = lax.broadcasted_iota(jnp.int32, (256, 256), 0)
    column = lax.broadcasted_iota(jnp.int32, (256, 256), 1)
    source = jnp.where(row < 128, 2 * row, 2 * row - 255)
    return jnp.where(column == source, 1.0, 0.0).astype(jnp.bfloat16)


def attend(stream, queries, keys_ref, values_ref, bias_ref, scores_ref, tokens):
    norm = stream * lax.rsqrt(jnp.mean(stream * stream, axis=1, keepdims=True) + EPS)
    query = (queries + norm).astype(jnp.bfloat16)
    count = GROUP * ROWS
    chunks = [(at, 256) for at in range(0, tokens, 256)] + [(tokens, HD)]
    top = jnp.full((count, HD), HIDDEN, jnp.float32)
    for at, size in chunks:
        part = contract_last(query, keys_ref[at : at + size, :])
        part = part.reshape(GROUP, ROWS, size) + bias_ref[:, at : at + size][None]
        part = part.reshape(count, size)
        scores_ref[:, at : at + size] = part
        for lane in range(0, size, HD):
            top = jnp.maximum(top, part[:, lane : lane + HD])
    top = jnp.max(top, axis=1, keepdims=True) * EXP2_SCALE
    total = jnp.zeros((count, HD), jnp.float32)
    mixed = jnp.zeros((count, HD), jnp.float32)
    for at, size in chunks:
        part = jnp.exp2(scores_ref[:, at : at + size] * EXP2_SCALE - top)
        for lane in range(0, size, HD):
            total = total + part[:, lane : lane + HD]
        mixed = mixed + jnp.dot(
            part.astype(jnp.bfloat16),
            values_ref[at : at + size, :],
            preferred_element_type=jnp.float32,
        )
    attended = (mixed / jnp.sum(total, axis=1, keepdims=True)).astype(jnp.bfloat16)
    return attended, (stream + attended.astype(jnp.float32)).astype(jnp.bfloat16)


def host_of(sections, heads, head, segment):
    columns = heads // 2
    x = lax.rem(head + segment, columns)
    z = lax.rem((sections // heads) * head + FIRST_HOST + lax.rem(x, 2), sections)
    return z, 2 * x + lax.rem(segment, 2)


def hosted_at(sections, heads, segments, z, tp):
    columns, stride = heads // 2, sections // heads
    x = tp // 2
    rest = lax.rem(z - FIRST_HOST - lax.rem(x, 2) + 2 * sections, sections)
    head = rest // stride
    segment = lax.rem(x - head + heads, columns)
    found = jnp.logical_and(lax.rem(rest, stride) == 0, segment < segments)
    found = jnp.logical_and(found, lax.rem(segment, 2) == lax.rem(tp, 2))
    return head, jnp.where(found, segment, -1)


def fused(
    sections,
    heads,
    pool_ref,
    queries_ref,
    new_ref,
    stream_ref,
    page_map_ref,
    counts_ref,
    fill_ref,
    out_ref,
    spare_ref,
    pages_ref,
    keys_ref,
    values_ref,
    bias_ref,
    scores_ref,
    asked,
    asking,
    opening,
    arrived,
    results,
    spare_send,
    spare_recv,
    page_send,
    page_recv,
    ask_send,
    ask_recv,
    open_send,
    stream_send,
    stream_recv,
    out_send,
    out_recv,
    near_sem,
    far_sem,
    all_sem,
):
    z, tp = lax.axis_index("section"), lax.axis_index("tp")
    me = z * heads + tp
    partner = tp + 1 - 2 * lax.rem(tp, 2)
    segments = len(STARTS) - 1
    depths = [STARTS[s + 1] - STARTS[s] for s in range(segments)]
    pages = sections * heads
    tokens = pages * PAGE
    count = GROUP * ROWS

    def place(other):
        return {"section": other[0], "tp": other[1]}

    def here(other):
        return jnp.logical_and(other[0] == z, other[1] == tp)

    def push(src, dst, send_sem, recv_sem, other):
        @pl.when(here(other))
        def _():
            pltpu.make_async_copy(src, dst, recv_sem).start()

        @pl.when(jnp.logical_not(here(other)))
        def _():
            pltpu.make_async_remote_copy(
                src_ref=src,
                dst_ref=dst,
                send_sem=send_sem,
                recv_sem=recv_sem,
                device_id=place(other),
                device_id_type=MESH,
            ).start()

    def wait_bytes(ref, sem):
        pltpu.make_async_copy(ref, ref, sem).wait()

    host = functools.partial(host_of, sections, heads)
    head, segment = hosted_at(sections, heads, segments, z, tp)
    other_segment = hosted_at(sections, heads, segments, z, partner)[1]
    hosting, helping = segment >= 0, other_segment >= 0
    start, depth = jnp.int32(0), jnp.int32(0)
    home_start, home_segment = jnp.int32(0), jnp.int32(0)
    for s in range(segments):
        start = jnp.where(segment == s, STARTS[s], start)
        depth = jnp.where(segment == s, depths[s], depth)
        home_start = jnp.where(z >= STARTS[s], STARTS[s], home_start)
        home_segment = jnp.where(z >= STARTS[s], s, home_segment)
    home_host, first_host = host(tp, home_segment), host(tp, 0)
    opens = z == first_host[0]

    reach = sections // 4

    def tell_row(sem):
        for d in range(1, heads):
            pl.semaphore_signal(
                sem, inc=1, device_id={"tp": lax.rem(tp + d, heads)}, device_id_type=MESH
            )

    barrier = pltpu.get_barrier_semaphore()
    for d in range(1, reach + 1):
        for other in (lax.rem(z + d, sections), lax.rem(z + sections - d, sections)):
            pl.semaphore_signal(
                barrier, inc=1, device_id={"section": other}, device_id_type=MESH
            )
    tell_row(barrier)
    opening[...] = by_group(stream_ref[...]).astype(jnp.bfloat16)
    asking[:count, :] = by_group(queries_ref[...]).astype(jnp.bfloat16)
    asking[count:, :] = new_ref[...]
    pl.semaphore_wait(barrier, heads - 1 + 2 * reach)
    tell_row(near_sem)
    for other in (lax.rem(z + reach, sections), lax.rem(z + sections - reach, sections)):
        pl.semaphore_signal(far_sem, inc=1, device_id={"section": other}, device_id_type=MESH)

    def spare(s):
        layers = pl.ds(STARTS[s], depths[s])
        return pltpu.make_async_remote_copy(
            src_ref=pool_ref.at[layers],
            dst_ref=spare_ref.at[layers],
            send_sem=spare_send.at[s],
            recv_sem=spare_recv.at[s],
            device_id={"tp": partner},
            device_id_type=MESH,
        )

    @pl.when(hosting)
    def _():
        for s in range(segments):
            spare(s).start()
            for j in range(depths[s]):

                @pl.when(segment == s)
                def _():
                    pltpu.make_async_copy(
                        pool_ref.at[STARTS[s] + j, head], pages_ref.at[j, me], page_recv.at[j]
                    ).start()

    def scatter(s, near, source_ref, owner):
        def step(i, carry):
            j = i // heads
            goal = lax.rem(z + tp + i, heads)
            other = host(goal, s)
            wanted = jnp.logical_not(jnp.logical_and(other[0] == z, other[1] == owner))
            if near is not None:
                ahead = lax.rem(other[0] - z + sections, sections)
                close = jnp.logical_or(ahead <= reach, ahead >= sections - reach)
                wanted = jnp.logical_and(wanted, close if near else jnp.logical_not(close))

            @pl.when(wanted)
            def _():
                pltpu.make_async_remote_copy(
                    src_ref=source_ref.at[STARTS[s] + j, goal],
                    dst_ref=pages_ref.at[j, z * heads + owner],
                    send_sem=page_send,
                    recv_sem=page_recv.at[j],
                    device_id=place(other),
                    device_id_type=MESH,
                ).start()

            return carry

        lax.fori_loop(0, depths[s] * heads, step, 0)

    pl.semaphore_wait(near_sem, heads - 1)
    pl.semaphore_wait(far_sem, 2)
    tell_row(all_sem)

    @pl.when(jnp.logical_not(hosting))
    def _():
        for s in range(NEAR_FIRST):
            scatter(s, True, pool_ref, tp)

    pl.semaphore_wait(all_sem, heads - 1)
    push(asking, asked.at[z - home_start], ask_send, ask_recv.at[z - home_start], home_host)

    @pl.when(opens)
    def _():
        push(opening, arrived, open_send, stream_recv, first_host)


    @pl.when(jnp.logical_not(hosting))
    def _():
        for s in range(segments):
            scatter(s, False if s < NEAR_FIRST else None, pool_ref, tp)

            @pl.when(helping)
            def _():
                spare(s).wait_recv()
                scatter(s, None, spare_ref, partner)

    @pl.when(hosting)
    def _():
        build_bias(page_map_ref, counts_ref, fill_ref, bias_ref, pages)
        part = parting()

        def prepare(j):
            wait_bytes(asked.at[j], ask_recv.at[j])
            wait_bytes(pages_ref.at[j], page_recv.at[j])
            for c in range(tokens // 128):
                per = 256 // (2 * PAGE)
                mixed = pages_ref[j, c * per : (c + 1) * per].reshape(256, HD)
                both = jnp.dot(part, mixed, preferred_element_type=jnp.float32)
                keys_ref[j, c * 128 : (c + 1) * 128, :] = both[:128].astype(jnp.bfloat16)
                values_ref[j, c * 128 : (c + 1) * 128, :] = both[128:].astype(jnp.bfloat16)
            both = jnp.dot(
                part[:, : 2 * ROWS], asked[j, count:, :], preferred_element_type=jnp.float32
            )
            keys_ref[j, tokens:, :] = both[:HD].astype(jnp.bfloat16)
            values_ref[j, tokens:, :] = both[HD:].astype(jnp.bfloat16)

        def run(j):
            attended, passed = attend(
                arrived[...].astype(jnp.float32),
                asked[j, :count, :].astype(jnp.float32),
                keys_ref.at[j],
                values_ref.at[j],
                bias_ref,
                scores_ref,
                tokens,
            )
            arrived[...] = passed
            results[j] = attended

        def deliver(j):
            push(results.at[j], out_ref, out_send.at[j], out_recv, (start + j, head))

        def where_deep(j, act):
            if j < min(depths):
                act(j)
            else:
                pl.when(depth > j)(functools.partial(act, j))

        for j in range(min(AHEAD, max(depths))):
            where_deep(j, prepare)

        onward = pltpu.make_async_remote_copy(
            src_ref=arrived,
            dst_ref=arrived,
            send_sem=stream_send,
            recv_sem=stream_recv,
            device_id=place(host(head, jnp.minimum(segment + 1, segments - 1))),
            device_id_type=MESH,
        )

        onward.wait_recv()

        def advance(j):
            if j >= AHEAD:
                prepare(j)
            run(j)

            @pl.when(jnp.logical_and(j == depth - 1, segment < segments - 1))
            def _():
                onward.start()

            deliver(j)

        for j in range(max(depths)):
            where_deep(j, advance)

        def drain(j):
            @pl.when(jnp.logical_not(here((start + j, head))))
            def _():
                wait_bytes(results.at[j], out_send.at[j])

        for j in range(max(depths)):
            where_deep(j, drain)

        @pl.when(segment < segments - 1)
        def _():
            wait_bytes(arrived, stream_send)

        for s in range(segments):
            spare(s).wait_send()

    wait_bytes(out_ref, out_recv)

    @pl.when(jnp.logical_not(here(home_host)))
    def _():
        wait_bytes(asking, ask_send)

    @pl.when(jnp.logical_and(opens, jnp.logical_not(here(first_host))))
    def _():
        wait_bytes(opening, open_send)

    @pl.when(jnp.logical_not(hosting))
    def _():
        wait_bytes(pool_ref, page_send)

        @pl.when(helping)
        def _():
            wait_bytes(pool_ref.at[pl.ds(0, sections - 1)], page_send)
            for s in range(segments):

                @pl.when(other_segment == s)
                def _():
                    wait_bytes(pool_ref.at[0, pl.ds(0, heads - depths[s])], page_send)


def shards(pool, queries, new_kv, stream_in, page_map, page_counts, last_fill):
    sections, heads = lax.axis_size("section"), lax.axis_size("tp")
    pages = page_map.shape[0]
    tokens = pages * PAGE
    segments = len(STARTS) - 1
    depth = max(STARTS[s + 1] - STARTS[s] for s in range(segments))
    count = GROUP * ROWS
    slots = pool.reshape(sections, heads, 2, PAGE, HD).transpose(0, 1, 3, 2, 4)
    slots = slots.reshape(sections, heads, 2 * PAGE, HD)
    vmem = pl.BlockSpec(memory_space=pltpu.VMEM)
    smem = pl.BlockSpec(memory_space=pltpu.SMEM)
    dma = pltpu.SemaphoreType.DMA
    half = jnp.bfloat16
    out = pl.pallas_call(
        lambda *refs: fused(sections, heads, *refs),
        out_shape=jax.ShapeDtypeStruct((count, HD), half),
        in_specs=[pl.BlockSpec(memory_space=pl.ANY)] + [vmem] * 4 + [smem] * 2,
        out_specs=vmem,
        scratch_shapes=[
            pltpu.VMEM((sections, heads, 2 * PAGE, HD), half),
            pltpu.VMEM((depth, pages, 2 * PAGE, HD), half),
            pltpu.VMEM((depth, tokens + HD, HD), half),
            pltpu.VMEM((depth, tokens + HD, HD), half),
            pltpu.VMEM((ROWS, tokens + HD), jnp.float32),
            pltpu.VMEM((count, tokens + HD), jnp.float32),
            pltpu.VMEM((depth, count + 2 * ROWS, HD), half),
            pltpu.VMEM((count + 2 * ROWS, HD), half),
            pltpu.VMEM((count, HD), half),
            pltpu.VMEM((count, HD), half),
            pltpu.VMEM((depth, count, HD), half),
            dma((segments,)),
            dma((segments,)),
            dma,
            dma((depth,)),
            dma,
            dma((depth,)),
            dma,
            dma,
            dma,
            dma((depth,)),
            dma,
            pltpu.SemaphoreType.REGULAR,
            pltpu.SemaphoreType.REGULAR,
            pltpu.SemaphoreType.REGULAR,
        ],
        compiler_params=pltpu.CompilerParams(
            collective_id=0, has_side_effects=True, vmem_limit_bytes=60 * 1024 * 1024
        ),
    )(
        slots,
        queries[0],
        new_kv.reshape(2 * ROWS, HD),
        stream_in,
        page_map.reshape(1, pages),
        page_counts,
        last_fill,
    )
    return out.reshape(GROUP, ROWS, HD).transpose(1, 0, 2).reshape(1, ROWS, GROUP * HD)


def solution(mesh):
    in_specs = (
        P(("rep", "section", "tp"), None, None, None),
        P("section", "rep", "tp"),
        P("section", "rep", None, "tp"),
        P("rep", "tp"),
        P("rep"),
        P("rep"),
        P("rep"),
    )
    out_specs = P("section", "rep", "tp")
    return jax.shard_map(shards, mesh=mesh, in_specs=in_specs, out_specs=out_specs, check_vma=False)
```
